32 devices in a mesh: groups: 2 (over x), tensor: 16 (over z, y, core).
Axes of the slice: x: 2, y: 2, z: 4, core: 2. Of those that a mesh axis runs over, the one named last changes fastest.
Arguments:
- tokens: bfloat16 [256, 4096], P(('groups', 'tensor')), parts along dimension 0, may hold values from -6 to 6
- cotangent: bfloat16 [256, 4096], P(('groups', 'tensor')), parts along dimension 0, may hold values from -6 to 6
- gate_weight: bfloat16 [4096, 16384], P(None, 'tensor'), may hold values from -0.09375 to 0.09375
- up_weight: bfloat16 [4096, 16384], P(None, 'tensor'), may hold values from -0.09375 to 0.09375
- down_weight: bfloat16 [16384, 4096], P('tensor'), may hold values from -0.046875 to 0.046875
- gate_mask: int32 [32, 128], P(None, 'tensor'), may hold values from 0 to 1, as said below
- up_mask: int32 [32, 128], P(None, 'tensor'), may hold values from 0 to 1, as said below
- down_mask: int32 [128, 32], P('tensor'), may hold values from 0 to 1, as said below
Outputs:
- mixed: bfloat16 [256, 4096], P(('groups', 'tensor')), parts along dimension 0
- grad_tokens: bfloat16 [256, 4096], P(('groups', 'tensor')), parts along dimension 0
- grad_gate: bfloat16 [8192, 16384], P('groups', 'tensor'), parts along dimension 0
- grad_up: bfloat16 [8192, 16384], P('groups', 'tensor'), parts along dimension 0
- grad_down: bfloat16 [32768, 4096], P(('groups', 'tensor')), parts along dimension 0
The draws below stay inside these ranges and needn't reach their ends.
There are 2 independent parts, one for each index of `groups`. The reference program is written for one: setup_inputs(seed, part) draws one part's arguments, and reference() takes and returns one part's arrays. A program takes and returns all parts, laid end to end along the dimension named above; an argument that names none is the same for every part. Nothing has to cross between parts.
Inputs may be any that keep to these rules, and one draw needn't show every extreme that they name: `gate_mask`: 0 or 1; the share of kept blocks differs from one column of blocks of hidden units to another. `up_mask`: 0 or 1; the share of kept blocks differs from one column of blocks of hidden units to another. `down_mask`: 0 or 1; the share of kept blocks differs from one row of blocks of hidden units to another.
All inputs are finite; a program needn't handle non-finite values.
Results may differ from the reference program's by a relative error of at most 0.0049.
Values may be sent and summed in bfloat16 or wider, within the bound.
A program may use at most 192 MiB of HBM per device.

```python
import jax
import jax.numpy as jnp

BLK = 128
D = 4096
FF = 16384
TOKENS = 128


def column_mask(key, rows, cols, along_rows):
    key_level, key_bits = jax.random.split(key)
    if along_rows:
        level = jax.random.randint(key_level, (rows, 1), 1, 9)
    else:
        level = jax.random.randint(key_level, (1, cols), 1, 9)
    bits = jax.random.randint(key_bits, (rows, cols), 0, 8)
    return (bits < level).astype(jnp.int32)


def draw_gate_mask(key, part):
    key = jax.random.fold_in(key, 11)
    return column_mask(key, D // BLK, FF // BLK, False)


def draw_up_mask(key, part):
    key = jax.random.fold_in(key, 23)
    return column_mask(key, D // BLK, FF // BLK, False)


def draw_down_mask(key, part):
    key = jax.random.fold_in(key, 37)
    return column_mask(key, FF // BLK, D // BLK, True)


def block_scale(own_key, dims, shards, least, high):
    level = 1.0
    for dim, parts in shards:
        heights = jax.random.uniform(jax.random.fold_in(jax.random.fold_in(own_key, 6), dim), (parts,), jnp.float32, least / len(shards), high / len(shards))
        level = level * jnp.repeat(jnp.exp(heights), dims[dim] // parts).reshape((-1,) + (1,) * (len(dims) - 1 - dim))
    return level


def gaussian(stream_key, shape, deviation, most, cuts=(), held_as=jnp.bfloat16):
    array = deviation * jax.random.normal(stream_key, shape, jnp.float32)
    if cuts:
        array = array * block_scale(stream_key, shape, cuts, -0.22, 0.18)
    return jnp.clip(array, -most, most).astype(held_as)


def setup_inputs(seed: int = 0, part: int = 0) -> dict:
    keys = jax.random.split(jax.random.key(seed), 9)
    part_keys = jax.random.split(jax.random.fold_in(keys[8], part), 9)
    tokens = gaussian(part_keys[0], (TOKENS, D), 1.0, 6.0, ((0, 16),))
    cotangent = gaussian(part_keys[1], (TOKENS, D), 1.0, 6.0, ((0, 16),))
    gate_weight = gaussian(keys[2], (D, FF), D ** -0.5, 0.09375, ((1, 16),))
    up_weight = gaussian(keys[3], (D, FF), D ** -0.5, 0.09375, ((1, 16),))
    down_weight = gaussian(keys[4], (FF, D), FF ** -0.5, 0.046875, ((0, 16),))
    gate_mask = draw_gate_mask(jax.random.fold_in(keys[8], 71), part)
    up_mask = draw_up_mask(jax.random.fold_in(keys[8], 71), part)
    down_mask = draw_down_mask(jax.random.fold_in(keys[8], 71), part)
    return {"tokens": tokens, "cotangent": cotangent, "gate_weight": gate_weight, "up_weight": up_weight, "down_weight": down_weight, "gate_mask": gate_mask, "up_mask": up_mask, "down_mask": down_mask}


def spread(mask):
    rows, cols = mask.shape
    return jnp.broadcast_to(mask[:, None, :, None], (rows, BLK, cols, BLK)).reshape(rows * BLK, cols * BLK)


def reference(tokens, cotangent, gate_weight, up_weight, down_weight, gate_mask, up_mask, down_mask):
    gate_full = spread(gate_mask)
    up_full = spread(up_mask)
    down_full = spread(down_mask)
    gate_kept = gate_weight * gate_full.astype(jnp.bfloat16)
    up_kept = up_weight * up_full.astype(jnp.bfloat16)
    down_kept = down_weight * down_full.astype(jnp.bfloat16)
    gate = jnp.dot(tokens, gate_kept, preferred_element_type=jnp.float32)
    up = jnp.dot(tokens, up_kept, preferred_element_type=jnp.float32)
    sig = jax.nn.sigmoid(gate)
    hidden = (gate * sig * up).astype(jnp.bfloat16)
    mixed = jnp.dot(hidden, down_kept, preferred_element_type=jnp.float32).astype(jnp.bfloat16)
    grad_hidden = jnp.dot(cotangent, down_kept.T, preferred_element_type=jnp.float32)
    grad_gate_pre = (grad_hidden * up * sig * (1.0 + gate * (1.0 - sig))).astype(jnp.bfloat16)
    grad_up_pre = (grad_hidden * gate * sig).astype(jnp.bfloat16)
    grad_tokens = (jnp.dot(grad_gate_pre, gate_kept.T, preferred_element_type=jnp.float32)
                   + jnp.dot(grad_up_pre, up_kept.T, preferred_element_type=jnp.float32)).astype(jnp.bfloat16)
    grad_gate = (jnp.dot(tokens.T, grad_gate_pre, preferred_element_type=jnp.float32) * gate_full.astype(jnp.float32)).astype(jnp.bfloat16)
    grad_up = (jnp.dot(tokens.T, grad_up_pre, preferred_element_type=jnp.float32) * up_full.astype(jnp.float32)).astype(jnp.bfloat16)
    grad_down = (jnp.dot(hidden.T, cotangent, preferred_element_type=jnp.float32) * down_full.astype(jnp.float32)).astype(jnp.bfloat16)
    return (mixed, grad_tokens, grad_gate, grad_up, grad_down)
```

```python
import functools

import jax
import jax.numpy as jnp
from jax import lax
from jax.experimental import pallas as pl
from jax.experimental.pallas import tpu as pltpu
from jax.sharding import PartitionSpec as P

BLK = 128
CHUNKS = 4
F32 = jnp.float32
BF16 = jnp.bfloat16


def dot(left, right, left_dim=1, right_dim=0):
    return lax.dot_general(
        left, right, (((left_dim,), (right_dim,)), ((), ())), preferred_element_type=F32
    )


def spread_lanes(mask, out):
    rows, cols = mask.shape
    for j in range(cols):
        out[:, j * BLK:(j + 1) * BLK] = jnp.broadcast_to(
            mask[:, j:j + 1].astype(F32), (rows, BLK)
        )


def masked(block, row):
    cols = block.shape[1]
    wide = jnp.broadcast_to(row, (16, cols)).astype(BF16)
    return (block.reshape(BLK // 16, 16, cols) * wide[None]).reshape(BLK, cols)


def exchange_kernel(
    m, tok, cot, gm, um, dm, gw_h, uw_h, dw_h,
    mixed_o, gt_o, xw, cw, hid, ggp, gup, eg, eu, ed,
    gw, uw, dw, tbuf, cbuf, gate, up, gh, gs, du,
    pb, ra, rb, bb, cb, rz, wsem, send_sem, recv_sem,
):
    n = 4 * m
    per, d = tok.shape
    half = d // 2
    hidden = gate.shape[1]
    total = gate.shape[0]
    kc_n = wsem.shape[1]
    kc = d // kc_n
    width = d // CHUNKS
    h = width // 2
    group = lax.axis_index("groups")
    t = lax.axis_index("tensor")
    c, y, z = lax.rem(t, 2), lax.rem(t // 2, 2), t // 4

    def device(cc, yy, zz):
        return (group, zz * 4 + yy * 2 + cc)

    def gate_copy(k):
        rows = pl.ds(pl.multiple_of(k * kc, kc), kc)
        return pltpu.make_async_copy(gw_h.at[rows, :], gw.at[rows, :], wsem.at[0, k])

    def up_copy(k):
        rows = pl.ds(pl.multiple_of(k * kc, kc), kc)
        return pltpu.make_async_copy(uw_h.at[rows, :], uw.at[rows, :], wsem.at[1, k])

    def down_copy(k):
        return pltpu.make_async_copy(
            dw_h.at[:, pl.ds(k * width, width)], dw.at[k], wsem.at[2, k]
        )

    for k in range(kc_n):
        gate_copy(k).start()
        up_copy(k).start()
    for k in range(CHUNKS):
        down_copy(k).start()

    z_peers = [lax.rem(z + off, m) for off in range(m)]
    z_from = [lax.rem(z - off + m, m) for off in range(m)]
    y_peer = device(c, 1 - y, z)
    c_peer = device(1 - c, y, z)

    barrier = pltpu.get_barrier_semaphore()
    peers = [device(c, y, z_peers[off]) for off in range(1, m)] + [y_peer, c_peer]
    for peer in peers:
        pl.semaphore_signal(barrier, inc=1, device_id=peer, device_id_type=pl.DeviceIdType.MESH)

    def own_slab(src, buf):
        v = src[...].astype(F32)
        buf[c, y, z] = jnp.concatenate([v[:, :half], v[:, half:]], axis=0).astype(BF16)

    own_slab(tok, tbuf)
    own_slab(cot, cbuf)
    spread_lanes(gm, eg)
    spread_lanes(um, eu)
    spread_lanes(dm, ed)
    pl.semaphore_wait(barrier, len(peers))

    counter = [0]
    sent = []

    def remote(src, dst, peer):
        i = counter[0]
        counter[0] += 1
        copy = pltpu.make_async_remote_copy(
            src_ref=src, dst_ref=dst, send_sem=send_sem.at[i], recv_sem=recv_sem.at[i],
            device_id=peer, device_id_type=pl.DeviceIdType.MESH,
        )
        sent.append(copy)
        return copy

    def gather(buf):
        own = buf.at[c, y, z]
        zc = [remote(own, own, device(c, y, z_peers[off])) for off in range(1, m)]
        yc = [remote(buf.at[c, y, s], buf.at[c, y, s], y_peer) for s in z_from]
        cc = [
            [remote(buf.at[c, yy, s], buf.at[c, yy, s], c_peer) for s in z_from]
            for yy in (y, 1 - y)
        ]

        def begin():
            for copy in zc:
                copy.start()
            yc[0].start()
            cc[0][0].start()

        def forward():
            for off in range(1, m):
                zc[off - 1].wait_recv()
                yc[off].start()
                cc[0][off].start()

        def across():
            for off in range(m):
                yc[off].wait_recv()
                cc[1][off].start()

        def end():
            for row in cc:
                for copy in row:
                    copy.wait_recv()

        return begin, forward, across, end

    def unpack(buf, out):
        for p in range(n // 2):
            a, b = (buf[q // (2 * m), (q // m) % 2, q % m].astype(F32) for q in (2 * p, 2 * p + 1))
            rows = slice(2 * per * p, 2 * per * (p + 1))
            out[rows, :half] = jnp.concatenate([a[:per], b[:per]], axis=0).astype(BF16)
            out[rows, half:] = jnp.concatenate([a[per:], b[per:]], axis=0).astype(BF16)

    t_begin, t_forward, t_across, t_end = gather(tbuf)
    c_begin, c_forward, c_across, c_end = gather(cbuf)
    t_begin()
    t_forward()
    c_begin()
    t_across()
    t_end()
    unpack(tbuf, xw)
    gate[...] = jnp.zeros_like(gate)
    up[...] = jnp.zeros_like(up)

    def first(k, carry):
        cols = pl.ds(pl.multiple_of(k * kc, kc), kc)
        gate_copy(k).wait()
        up_copy(k).wait()
        x = xw[:, cols]
        for w, e, acc in ((gw, eg, gate), (uw, eu, up)):
            for b in range(kc // BLK):
                rows = pl.ds(pl.multiple_of(k * kc + b * BLK, BLK), BLK)
                w[rows, :] = masked(w[rows, :], e[pl.ds(k * (kc // BLK) + b, 1), :])
            acc[...] += dot(x, w[cols, :])
        return carry

    lax.fori_loop(0, kc_n // 2, first, 0)
    c_forward()
    lax.fori_loop(kc_n // 2, kc_n, first, 0)
    c_across()

    step = 32

    def middle(k, carry):
        rows = pl.ds(pl.multiple_of(k * step, step), step)
        g, u = gate[rows, :], up[rows, :]
        s = jax.nn.sigmoid(g)
        a = g * s
        gs[rows, :] = a
        hid[rows, :] = (a * u).astype(BF16)
        du[rows, :] = u * s * (1.0 + g * (1.0 - s))
        return carry

    lax.fori_loop(0, total // step, middle, 0)
    c_end()
    unpack(cbuf, cw)

    sums = []

    def scatter_begin(which, k, low, high):
        parts = jnp.concatenate([low.reshape(n, per, h), high.reshape(n, per, h)], axis=1)
        pb[which, k] = parts.astype(BF16).reshape(2, 2, m, 2 * per, h)
        a = remote(pb.at[which, k, 1 - c], ra.at[which, k], c_peer)
        b = remote(bb.at[which, k], rb.at[which, k], y_peer)
        zs = [
            remote(cb.at[which, k, z_peers[off]], rz.at[which, k, off - 1], device(c, y, z_peers[off]))
            for off in range(1, m)
        ]
        a.start()

        def second():
            a.wait_recv()
            bb[which, k] = (pb[which, k, c, 1 - y].astype(F32) + ra[which, k, 1 - y].astype(F32)).astype(BF16)
            b.start()

        def third():
            b.wait_recv()
            cb[which, k] = (
                pb[which, k, c, y].astype(F32) + ra[which, k, y].astype(F32) + rb[which, k].astype(F32)
            ).astype(BF16)
            for copy in zs:
                copy.start()

        def last():
            value = (
                pb[which, k, c, y, z].astype(F32) + ra[which, k, y, z].astype(F32) + rb[which, k, z].astype(F32)
            )
            for off in range(1, m):
                zs[off - 1].wait_recv()
                value = value + rz[which, k, off - 1].astype(F32)
            out = gt_o if which else mixed_o
            out[:, k * width:k * width + h] = value[:per].astype(BF16)
            out[:, k * width + h:(k + 1) * width] = value[per:].astype(BF16)

        sums.append((second, third, last))

    def advance(i):
        for stage in range(3):
            j = i - 1 - stage
            if 0 <= j < 2 * CHUNKS:
                sums[j][stage]()

    for k in range(CHUNKS):
        down_copy(k).wait()
        cols = slice(k * width, (k + 1) * width)
        for j in range(hidden // BLK):
            rows = slice(j * BLK, (j + 1) * BLK)
            dw[k, rows, :] = masked(dw[k, rows, :], ed[j:j + 1, cols])
        hv = hid[...]
        scatter_begin(0, k, dot(hv, dw[k, :, :h]), dot(hv, dw[k, :, h:]))
        value = dot(cw[:, cols], dw[k], 1, 1)
        gh[...] = value if k == 0 else gh[...] + value
        advance(k)

    def pre(k, carry):
        rows = pl.ds(pl.multiple_of(k * step, step), step)
        g = gh[rows, :]
        ggp[rows, :] = (g * du[rows, :]).astype(BF16)
        gup[rows, :] = (g * gs[rows, :]).astype(BF16)
        return carry

    lax.fori_loop(0, total // step, pre, 0)

    for k in range(CHUNKS):
        a, b = ggp[...], gup[...]
        halves = []
        for o in (k * width, k * width + h):
            halves.append(dot(a, gw[o:o + h, :], 1, 1) + dot(b, uw[o:o + h, :], 1, 1))
        scatter_begin(1, k, *halves)
        advance(CHUNKS + k)
    for i in range(2 * CHUNKS, 2 * CHUNKS + 4):
        advance(i)
    for copy in sent:
        copy.wait_send()


def grads_kernel(xw, cw, hid, ggp, gup, eg, eu, ed, gg, gu, gd):
    i = pl.program_id(0)
    block = xw.shape[1]
    for pre, e, out in ((ggp, eg, gg), (gup, eu, gu)):
        for b in range(block // BLK):
            rows = slice(b * BLK, (b + 1) * BLK)
            value = dot(xw[:, rows], pre[...], 0, 0)
            out[rows, :] = (value * e[pl.ds(i * (block // BLK) + b, 1), :]).astype(BF16)
    for j in range(hid.shape[1] // BLK):
        rows = slice(j * BLK, (j + 1) * BLK)
        value = dot(hid[:, rows], cw[...], 0, 0)
        gd[rows, :] = (value * ed[j:j + 1, :]).astype(BF16)


def shards(n, tokens, cotangent, gate_weight, up_weight, down_weight, gate_mask, up_mask, down_mask):
    m = n // 4
    per, d = tokens.shape
    total = n * per
    hidden = gate_weight.shape[1]
    width = d // CHUNKS
    h = width // 2
    kc_n = 8
    copies = 2 * (m - 1 + 3 * m) + 2 * CHUNKS * (m + 1)
    vmem = pl.BlockSpec(memory_space=pltpu.VMEM)
    hbm = pl.BlockSpec(memory_space=pl.ANY)
    shape = jax.ShapeDtypeStruct
    mixed, grad_tokens, xw, cw, hid, ggp, gup, eg, eu, ed = pl.pallas_call(
        functools.partial(exchange_kernel, m),
        out_shape=(
            shape((per, d), BF16), shape((per, d), BF16),
            shape((total, d), BF16), shape((total, d), BF16),
            shape((total, hidden), BF16), shape((total, hidden), BF16), shape((total, hidden), BF16),
            shape((d // BLK, hidden), F32), shape((d // BLK, hidden), F32),
            shape((hidden // BLK, d), F32),
        ),
        in_specs=[vmem] * 5 + [hbm] * 3,
        out_specs=(vmem,) * 10,
        scratch_shapes=[
            pltpu.VMEM((d, hidden), BF16), pltpu.VMEM((d, hidden), BF16),
            pltpu.VMEM((CHUNKS, hidden, width), BF16),
            pltpu.VMEM((2, 2, m, 2 * per, d // 2), BF16), pltpu.VMEM((2, 2, m, 2 * per, d // 2), BF16),
            *[pltpu.VMEM((total, hidden), F32)] * 5,
            pltpu.VMEM((2, CHUNKS, 2, 2, m, 2 * per, h), BF16),
            pltpu.VMEM((2, CHUNKS, 2, m, 2 * per, h), BF16),
            pltpu.VMEM((2, CHUNKS, m, 2 * per, h), BF16),
            pltpu.VMEM((2, CHUNKS, m, 2 * per, h), BF16),
            pltpu.VMEM((2, CHUNKS, m, 2 * per, h), BF16),
            pltpu.VMEM((2, CHUNKS, m - 1, 2 * per, h), BF16),
            pltpu.SemaphoreType.DMA((3, kc_n)),
            pltpu.SemaphoreType.DMA((copies,)),
            pltpu.SemaphoreType.DMA((copies,)),
        ],
        compiler_params=pltpu.CompilerParams(
            collective_id=0, has_side_effects=True, vmem_limit_bytes=60 * 2**20
        ),
        cost_estimate=pl.CostEstimate(
            flops=12 * total * d * hidden, bytes_accessed=6 * d * hidden, transcendentals=total * hidden
        ),
    )(tokens, cotangent, gate_mask, up_mask, down_mask, gate_weight, up_weight, down_weight)

    block = 512
    whole = lambda *dims: pl.BlockSpec(dims, lambda i: (0, 0))
    grad_gate, grad_up, grad_down = pl.pallas_call(
        grads_kernel,
        grid=(d // block,),
        out_shape=(shape((d, hidden), BF16), shape((d, hidden), BF16), shape((hidden, d), BF16)),
        in_specs=[
            pl.BlockSpec((total, block), lambda i: (0, i)),
            pl.BlockSpec((total, block), lambda i: (0, i)),
            whole(total, hidden), whole(total, hidden), whole(total, hidden),
            whole(d // BLK, hidden), whole(d // BLK, hidden),
            pl.BlockSpec((hidden // BLK, block), lambda i: (0, i)),
        ],
        out_specs=(
            pl.BlockSpec((block, hidden), lambda i: (i, 0)),
            pl.BlockSpec((block, hidden), lambda i: (i, 0)),
            pl.BlockSpec((hidden, block), lambda i: (0, i)),
        ),
        compiler_params=pltpu.CompilerParams(vmem_limit_bytes=32 * 2**20),
        cost_estimate=pl.CostEstimate(
            flops=6 * total * d * hidden, bytes_accessed=6 * d * hidden, transcendentals=0
        ),
    )(xw, cw, hid, ggp, gup, eg, eu, ed)
    return mixed, grad_tokens, grad_gate, grad_up, grad_down


def solution(mesh):
    return jax.shard_map(
        functools.partial(shards, mesh.shape["tensor"]),
        mesh=mesh,
        in_specs=(
            P(("groups", "tensor"), None),
            P(("groups", "tensor"), None),
            P(None, "tensor"),
            P(None, "tensor"),
            P("tensor", None),
            P(None, "tensor"),
            P(None, "tensor"),
            P("tensor", None),
        ),
        out_specs=(
            P(("groups", "tensor"), None),
            P(("groups", "tensor"), None),
            P("groups", "tensor"),
            P("groups", "tensor"),
            P(("groups", "tensor"), None),
        ),
        check_vma=False,
    )
```

```python
import functools

import jax
import jax.numpy as jnp
from jax import lax
from jax.experimental import pallas as pl
from jax.experimental.pallas import tpu as pltpu
from jax.sharding import PartitionSpec as P

BLK = 128
CHUNKS = 4
F32 = jnp.float32
BF16 = jnp.bfloat16


def dot(left, right, left_dim=1, right_dim=0):
    return lax.dot_general(
        left, right, (((left_dim,), (right_dim,)), ((), ())), preferred_element_type=F32
    )


def masked(block, keep):
    cols = block.shape[1]
    wide = jnp.concatenate([jnp.full((16, BLK), v, jnp.int32).astype(F32).astype(BF16) for v in keep], axis=1)
    return (block.reshape(BLK // 16, 16, cols) * wide[None]).reshape(BLK, cols)


def exchange_kernel(
    m, tok, cot, gm, um, dm, gw_h, uw_h, dw_h,
    mixed_o, gt_o, xw_o, cw_o, hid_o, ggp_o, gup_o,
    xw, cw, hid, ggp, gup, gw, uw, dw, tbuf, cbuf, gate, up, gh, gs, du,
    pb, ra, rb, bb, cb, rz, wsem, osem, send_sem, recv_sem,
):
    n = 4 * m
    per, d = tok.shape
    half = d // 2
    hidden = gate.shape[1]
    total = gate.shape[0]
    kc_n = wsem.shape[1]
    kc = d // kc_n
    width = d // CHUNKS
    h = width // 2
    group = lax.axis_index("groups")
    t = lax.axis_index("tensor")
    c, y, z = lax.rem(t, 2), lax.rem(t // 2, 2), t // 4

    def device(cc, yy, zz):
        return (group, zz * 4 + yy * 2 + cc)

    def gate_copy(k):
        rows = pl.ds(pl.multiple_of(k * kc, kc), kc)
        return pltpu.make_async_copy(gw_h.at[rows, :], gw.at[rows, :], wsem.at[0, k])

    def up_copy(k):
        rows = pl.ds(pl.multiple_of(k * kc, kc), kc)
        return pltpu.make_async_copy(uw_h.at[rows, :], uw.at[rows, :], wsem.at[1, k])

    def down_copy(k):
        return pltpu.make_async_copy(
            dw_h.at[:, pl.ds(k * width, width)], dw.at[k], wsem.at[2, k]
        )

    for k in range(kc_n):
        gate_copy(k).start()
        up_copy(k).start()
    for k in range(CHUNKS):
        down_copy(k).start()

    z_peers = [lax.rem(z + off, m) for off in range(m)]
    z_from = [lax.rem(z - off + m, m) for off in range(m)]
    y_peer = device(c, 1 - y, z)
    c_peer = device(1 - c, y, z)

    barrier = pltpu.get_barrier_semaphore()
    peers = [device(c, y, z_peers[off]) for off in range(1, m)] + [y_peer, c_peer]
    for peer in peers:
        pl.semaphore_signal(barrier, inc=1, device_id=peer, device_id_type=pl.DeviceIdType.MESH)

    def own_slab(src, buf):
        v = src[...].astype(F32)
        buf[c, y, z] = jnp.concatenate([v[:, :half], v[:, half:]], axis=0).astype(BF16)

    own_slab(tok, tbuf)
    own_slab(cot, cbuf)
    pl.semaphore_wait(barrier, len(peers))

    def save(i):
        src, dst = ((xw, xw_o), (cw, cw_o), (hid, hid_o), (ggp, ggp_o), (gup, gup_o))[i]
        return pltpu.make_async_copy(src, dst, osem.at[i])

    counter = [0]
    sent = []

    def remote(src, dst, peer):
        i = counter[0]
        counter[0] += 1
        copy = pltpu.make_async_remote_copy(
            src_ref=src, dst_ref=dst, send_sem=send_sem.at[i], recv_sem=recv_sem.at[i],
            device_id=peer, device_id_type=pl.DeviceIdType.MESH,
        )
        sent.append(copy)
        return copy

    def gather(buf):
        own = buf.at[c, y, z]
        zc = [remote(own, own, device(c, y, z_peers[off])) for off in range(1, m)]
        yc = [remote(buf.at[c, y, s], buf.at[c, y, s], y_peer) for s in z_from]
        cc = [
            [remote(buf.at[c, yy, s], buf.at[c, yy, s], c_peer) for s in z_from]
            for yy in (y, 1 - y)
        ]

        def begin():
            for copy in zc:
                copy.start()
            yc[0].start()
            cc[0][0].start()

        def forward():
            for off in range(1, m):
                zc[off - 1].wait_recv()
                yc[off].start()
                cc[0][off].start()

        def across():
            for off in range(m):
                yc[off].wait_recv()
                cc[1][off].start()

        def end():
            for row in cc:
                for copy in row:
                    copy.wait_recv()

        return begin, forward, across, end

    def unpack(buf, out):
        for p in range(n // 2):
            a, b = (buf[q // (2 * m), (q // m) % 2, q % m].astype(F32) for q in (2 * p, 2 * p + 1))
            rows = slice(2 * per * p, 2 * per * (p + 1))
            out[rows, :half] = jnp.concatenate([a[:per], b[:per]], axis=0).astype(BF16)
            out[rows, half:] = jnp.concatenate([a[per:], b[per:]], axis=0).astype(BF16)

    t_begin, t_forward, t_across, t_end = gather(tbuf)
    c_begin, c_forward, c_across, c_end = gather(cbuf)
    t_begin()
    t_forward()
    c_begin()
    t_across()
    t_end()
    unpack(tbuf, xw)
    save(0).start()
    gate[...] = jnp.zeros_like(gate)
    up[...] = jnp.zeros_like(up)

    def first(k, carry):
        cols = pl.ds(pl.multiple_of(k * kc, kc), kc)
        gate_copy(k).wait()
        up_copy(k).wait()
        x = xw[:, cols]
        for w, e, acc in ((gw, gm, gate), (uw, um, up)):
            for b in range(kc // BLK):
                rows = pl.ds(pl.multiple_of(k * kc + b * BLK, BLK), BLK)
                w[rows, :] = masked(
                    w[rows, :], [e[j, k * (kc // BLK) + b] for j in range(hidden // BLK)]
                )
            acc[...] += dot(x, w[cols, :])
        return carry

    lax.fori_loop(0, kc_n // 2, first, 0)
    c_forward()
    lax.fori_loop(kc_n // 2, kc_n, first, 0)
    c_across()

    step = 32

    def middle(k, carry):
        rows = pl.ds(pl.multiple_of(k * step, step), step)
        g, u = gate[rows, :], up[rows, :]
        s = jax.nn.sigmoid(g)
        a = g * s
        gs[rows, :] = a
        hid[rows, :] = (a * u).astype(BF16)
        du[rows, :] = u * s * (1.0 + g * (1.0 - s))
        return carry

    lax.fori_loop(0, total // step, middle, 0)
    c_end()
    unpack(cbuf, cw)
    save(1).start()
    save(2).start()

    sums = []

    def scatter_begin(which, k, low, high):
        parts = jnp.concatenate([low.reshape(n, per, h), high.reshape(n, per, h)], axis=1)
        pb[which, k] = parts.astype(BF16).reshape(2, 2, m, 2 * per, h)
        a = remote(pb.at[which, k, 1 - c], ra.at[which, k], c_peer)
        b = remote(bb.at[which, k], rb.at[which, k], y_peer)
        zs = [
            remote(cb.at[which, k, z_peers[off]], rz.at[which, k, off - 1], device(c, y, z_peers[off]))
            for off in range(1, m)
        ]
        a.start()

        def second():
            a.wait_recv()
            bb[which, k] = (pb[which, k, c, 1 - y].astype(F32) + ra[which, k, 1 - y].astype(F32)).astype(BF16)
            b.start()

        def third():
            b.wait_recv()
            cb[which, k] = (
                pb[which, k, c, y].astype(F32) + ra[which, k, y].astype(F32) + rb[which, k].astype(F32)
            ).astype(BF16)
            for copy in zs:
                copy.start()

        def last():
            value = (
                pb[which, k, c, y, z].astype(F32) + ra[which, k, y, z].astype(F32) + rb[which, k, z].astype(F32)
            )
            for off in range(1, m):
                zs[off - 1].wait_recv()
                value = value + rz[which, k, off - 1].astype(F32)
            out = gt_o if which else mixed_o
            out[:, k * width:k * width + h] = value[:per].astype(BF16)
            out[:, k * width + h:(k + 1) * width] = value[per:].astype(BF16)

        sums.append((second, third, last))

    def advance(i):
        for stage in range(2):
            j = i - 1 - stage
            if 0 <= j < 2 * CHUNKS:
                sums[j][stage]()

    for k in range(CHUNKS):
        down_copy(k).wait()
        cols = slice(k * width, (k + 1) * width)
        for j in range(hidden // BLK):
            rows = slice(j * BLK, (j + 1) * BLK)
            dw[k, rows, :] = masked(
                dw[k, rows, :], [dm[j, k * (width // BLK) + b] for b in range(width // BLK)]
            )
        hv = hid[...]
        scatter_begin(0, k, dot(hv, dw[k, :, :h]), dot(hv, dw[k, :, h:]))
        value = dot(cw[:, cols], dw[k], 1, 1)
        gh[...] = value if k == 0 else gh[...] + value
        advance(k)

    def pre(k, carry):
        rows = pl.ds(pl.multiple_of(k * step, step), step)
        g = gh[rows, :]
        ggp[rows, :] = (g * du[rows, :]).astype(BF16)
        gup[rows, :] = (g * gs[rows, :]).astype(BF16)
        return carry

    lax.fori_loop(0, total // step, pre, 0)
    save(3).start()
    save(4).start()

    for k in range(CHUNKS):
        a, b = ggp[...], gup[...]
        halves = []
        for o in (k * width, k * width + h):
            halves.append(dot(a, gw[o:o + h, :], 1, 1) + dot(b, uw[o:o + h, :], 1, 1))
        scatter_begin(1, k, *halves)
        advance(CHUNKS + k)
    for i in range(2 * CHUNKS, 2 * CHUNKS + 2):
        advance(i)
    for stages in sums:
        stages[2]()
    for copy in sent:
        copy.wait_send()
    for i in range(5):
        save(i).wait()


def grads_kernel(xw, cw, hid, ggp, gup, gm, um, dm, mixed, gt, gg, gu, gd, mixed_o, gt_o):
    i = pl.program_id(0)
    block = xw.shape[1]
    count = block // BLK

    @pl.when(i == 0)
    def _():
        mixed_o[...] = mixed[...]
        gt_o[...] = gt[...]

    def keep(value, scalars):
        wide = [jnp.full((8, BLK), v, jnp.int32).astype(F32) for v in scalars]
        wide = jnp.concatenate(wide, axis=1)
        cols = wide.shape[1]
        return (value.reshape(BLK // 8, 8, cols) * wide[None]).reshape(BLK, cols).astype(BF16)

    for pre, e, out in ((ggp, gm, gg), (gup, um, gu)):
        for b in range(count):
            rows = slice(b * BLK, (b + 1) * BLK)
            value = dot(xw[:, rows], pre[...], 0, 0)
            out[rows, :] = keep(value, [e[j, i * count + b] for j in range(e.shape[0])])
    for j in range(dm.shape[0]):
        rows = slice(j * BLK, (j + 1) * BLK)
        value = dot(hid[:, rows], cw[...], 0, 0)
        gd[rows, :] = keep(value, [dm[j, i * count + b] for b in range(count)])


def shards(n, tokens, cotangent, gate_weight, up_weight, down_weight, gate_mask, up_mask, down_mask):
    m = n // 4
    per, d = tokens.shape
    total = n * per
    hidden = gate_weight.shape[1]
    width = d // CHUNKS
    h = width // 2
    kc_n = 8
    copies = 2 * (m - 1 + 3 * m) + 2 * CHUNKS * (m + 1)
    vmem = pl.BlockSpec(memory_space=pltpu.VMEM)
    hbm = pl.BlockSpec(memory_space=pl.ANY)
    smem = pl.BlockSpec(memory_space=pltpu.SMEM)
    gate_mask, up_mask = gate_mask.T, up_mask.T
    shape = jax.ShapeDtypeStruct
    mixed, grad_tokens, xw, cw, hid, ggp, gup = pl.pallas_call(
        functools.partial(exchange_kernel, m),
        out_shape=(
            shape((per, d), BF16), shape((per, d), BF16),
            shape((total, d), BF16), shape((total, d), BF16),
            shape((total, hidden), BF16), shape((total, hidden), BF16), shape((total, hidden), BF16),
        ),
        in_specs=[vmem] * 2 + [smem] * 3 + [hbm] * 3,
        out_specs=(vmem,) * 2 + (hbm,) * 5,
        scratch_shapes=[
            *[pltpu.VMEM((total, d), BF16)] * 2, *[pltpu.VMEM((total, hidden), BF16)] * 3,
            pltpu.VMEM((d, hidden), BF16), pltpu.VMEM((d, hidden), BF16),
            pltpu.VMEM((CHUNKS, hidden, width), BF16),
            pltpu.VMEM((2, 2, m, 2 * per, d // 2), BF16), pltpu.VMEM((2, 2, m, 2 * per, d // 2), BF16),
            *[pltpu.VMEM((total, hidden), F32)] * 5,
            pltpu.VMEM((2, CHUNKS, 2, 2, m, 2 * per, h), BF16),
            pltpu.VMEM((2, CHUNKS, 2, m, 2 * per, h), BF16),
            pltpu.VMEM((2, CHUNKS, m, 2 * per, h), BF16),
            pltpu.VMEM((2, CHUNKS, m, 2 * per, h), BF16),
            pltpu.VMEM((2, CHUNKS, m, 2 * per, h), BF16),
            pltpu.VMEM((2, CHUNKS, m - 1, 2 * per, h), BF16),
            pltpu.SemaphoreType.DMA((3, kc_n)),
            pltpu.SemaphoreType.DMA((5,)),
            pltpu.SemaphoreType.DMA((copies,)),
            pltpu.SemaphoreType.DMA((copies,)),
        ],
        compiler_params=pltpu.CompilerParams(
            collective_id=0, has_side_effects=True, vmem_limit_bytes=60 * 2**20
        ),
        cost_estimate=pl.CostEstimate(
            flops=12 * total * d * hidden, bytes_accessed=6 * d * hidden, transcendentals=total * hidden
        ),
    )(tokens, cotangent, gate_mask, up_mask, down_mask, gate_weight, up_weight, down_weight)

    block = 512
    whole = lambda *dims: pl.BlockSpec(dims, lambda i: (0, 0))
    grad_gate, grad_up, grad_down, mixed, grad_tokens = pl.pallas_call(
        grads_kernel,
        grid=(d // block,),
        out_shape=(shape((d, hidden), BF16), shape((d, hidden), BF16), shape((hidden, d), BF16),
                   shape((per, d), BF16), shape((per, d), BF16)),
        in_specs=[
            pl.BlockSpec((total, block), lambda i: (0, i)),
            pl.BlockSpec((total, block), lambda i: (0, i)),
            whole(total, hidden), whole(total, hidden), whole(total, hidden),
            smem, smem, smem, whole(per, d), whole(per, d),
        ],
        out_specs=(
            pl.BlockSpec((block, hidden), lambda i: (i, 0)),
            pl.BlockSpec((block, hidden), lambda i: (i, 0)),
            pl.BlockSpec((hidden, block), lambda i: (0, i)),
            whole(per, d), whole(per, d),
        ),
        compiler_params=pltpu.CompilerParams(vmem_limit_bytes=60 * 2**20),
        cost_estimate=pl.CostEstimate(
            flops=6 * total * d * hidden, bytes_accessed=6 * d * hidden, transcendentals=0
        ),
    )(xw, cw, hid, ggp, gup, gate_mask, up_mask, down_mask, mixed, grad_tokens)
    return mixed, grad_tokens, grad_gate, grad_up, grad_down


def solution(mesh):
    return jax.shard_map(
        functools.partial(shards, mesh.shape["tensor"]),
        mesh=mesh,
        in_specs=(
            P(("groups", "tensor"), None),
            P(("groups", "tensor"), None),
            P(None, "tensor"),
            P(None, "tensor"),
            P("tensor", None),
            P(None, "tensor"),
            P(None, "tensor"),
            P("tensor", None),
        ),
        out_specs=(
            P(("groups", "tensor"), None),
            P(("groups", "tensor"), None),
            P("groups", "tensor"),
            P("groups", "tensor"),
            P(("groups", "tensor"), None),
        ),
        check_vma=False,
    )
```

```python
import functools

import jax
import jax.numpy as jnp
from jax import lax
from jax.experimental import pallas as pl
from jax.experimental.pallas import tpu as pltpu
from jax.sharding import PartitionSpec as P

BLK = 128
CHUNKS = 4
F32 = jnp.float32
BF16 = jnp.bfloat16


def dot(left, right, left_dim=1, right_dim=0):
    return lax.dot_general(
        left, right, (((left_dim,), (right_dim,)), ((), ())), preferred_element_type=F32
    )


def masked(block, keep):
    cols = block.shape[1]
    wide = jnp.concatenate([jnp.full((16, BLK), v, jnp.int32).astype(F32).astype(BF16) for v in keep], axis=1)
    return (block.reshape(BLK // 16, 16, cols) * wide[None]).reshape(BLK, cols)


def exchange_kernel(
    m, tok, cot, gm, um, dm, gw_h, uw_h, dw_h,
    mixed_o, gt_o, xw_o, cw_o, hid_o, ggp_o, gup_o,
    xw, cw, hid, ggp, gup, gw, uw, dw, tbuf, cbuf, gate, up, gh, gs, du,
    pb, ra, rb, bb, cb, rz, wsem, osem, send_sem, recv_sem,
):
    n = 4 * m
    per, d = tok.shape
    half = d // 2
    hidden = gate.shape[1]
    total = gate.shape[0]
    kc_n = wsem.shape[1]
    kc = d // kc_n
    width = d // CHUNKS
    h = width // 2
    group = lax.axis_index("groups")
    t = lax.axis_index("tensor")
    c, y, z = lax.rem(t, 2), lax.rem(t // 2, 2), t // 4

    def device(cc, yy, zz):
        return (group, zz * 4 + yy * 2 + cc)

    def gate_copy(k):
        rows = pl.ds(pl.multiple_of(k * kc, kc), kc)
        return pltpu.make_async_copy(gw_h.at[rows, :], gw.at[rows, :], wsem.at[0, k])

    def up_copy(k):
        rows = pl.ds(pl.multiple_of(k * kc, kc), kc)
        return pltpu.make_async_copy(uw_h.at[rows, :], uw.at[rows, :], wsem.at[1, k])

    def down_copy(k):
        return pltpu.make_async_copy(
            dw_h.at[:, pl.ds(k * width, width)], dw.at[k], wsem.at[2, k]
        )

    for k in range(kc_n):
        gate_copy(k).start()
        up_copy(k).start()
    for k in range(CHUNKS):
        down_copy(k).start()

    z_peers = [lax.rem(z + off, m) for off in range(m)]
    y_peer = device(c, 1 - y, z)
    c_peer = device(1 - c, y, z)

    barrier = pltpu.get_barrier_semaphore()
    peers = [device(c, y, z_peers[off]) for off in range(1, m)] + [y_peer, c_peer]
    for peer in peers:
        pl.semaphore_signal(barrier, inc=1, device_id=peer, device_id_type=pl.DeviceIdType.MESH)

    def own_slab(src, buf):
        v = src[...].astype(F32)
        buf[c, y, z] = jnp.concatenate([v[:, :half], v[:, half:]], axis=0).astype(BF16)

    own_slab(tok, tbuf)
    own_slab(cot, cbuf)
    pl.semaphore_wait(barrier, len(peers))

    def save(i):
        src, dst = ((xw, xw_o), (cw, cw_o), (hid, hid_o), (ggp, ggp_o), (gup, gup_o))[i]
        return pltpu.make_async_copy(src, dst, osem.at[i])

    counter = [0]
    sent = []

    def when(ok, act):
        if ok is None:
            act()
        else:
            pl.when(ok)(lambda: act())

    def remote(src, dst, peer, ok=None):
        i = counter[0]
        counter[0] += 1
        copy = pltpu.make_async_remote_copy(
            src_ref=src, dst_ref=dst, send_sem=send_sem.at[i], recv_sem=recv_sem.at[i],
            device_id=peer, device_id_type=pl.DeviceIdType.MESH,
        )
        sent.append((copy, ok))
        return copy

    right, left = device(c, y, jnp.minimum(z + 1, m - 1)), device(c, y, jnp.maximum(z - 1, 0))

    def gather(buf):
        slabs = [(None, z)]
        hops = {}
        for s in range(1, m):
            old_r, old_l = jnp.maximum(z - s + 1, 0), jnp.minimum(z + s - 1, m - 1)
            going = None if s == 1 else z - s + 1 >= 0
            coming = None if s == 1 else z + s - 1 < m
            to_right = z + 1 < m if going is None else jnp.logical_and(z + 1 < m, going)
            to_left = z >= 1 if coming is None else jnp.logical_and(z >= 1, coming)
            hops[s] = (
                remote(buf.at[c, y, old_r], buf.at[c, y, old_r], right, to_right), to_right,
                remote(buf.at[c, y, old_l], buf.at[c, y, old_l], left, to_left), to_left,
            )
            slabs.append((z - s >= 0, jnp.maximum(z - s, 0)))
            slabs.append((z + s < m, jnp.minimum(z + s, m - 1)))
        yc = [remote(buf.at[c, y, s], buf.at[c, y, s], y_peer, ok) for ok, s in slabs]
        cc = [
            [remote(buf.at[c, yy, s], buf.at[c, yy, s], c_peer, ok) for ok, s in slabs]
            for yy in (y, 1 - y)
        ]

        def hop(s):
            if s < m:
                when(hops[s][1], hops[s][0].start)
                when(hops[s][3], hops[s][2].start)

        def begin():
            hop(1)
            yc[0].start()
            cc[0][0].start()

        def forward():
            for s in range(1, m):
                for way in range(2):
                    i = 2 * s - 1 + way

                    def arrive(i=i, s=s, way=way):
                        hops[s][2 * way].wait_recv()

                    when(slabs[i][0], arrive)
                    if s + 1 < m:
                        when(hops[s + 1][2 * way + 1], hops[s + 1][2 * way].start)
                    when(slabs[i][0], yc[i].start)
                    when(slabs[i][0], cc[0][i].start)

        def across():
            for i, (ok, _) in enumerate(slabs):
                when(ok, yc[i].wait_recv)
                when(ok, cc[1][i].start)

        def end():
            for row in cc:
                for copy, (ok, _) in zip(row, slabs):
                    when(ok, copy.wait_recv)

        return begin, forward, across, end

    def unpack(buf, out):
        for p in range(n // 2):
            a, b = (buf[q // (2 * m), (q // m) % 2, q % m].astype(F32) for q in (2 * p, 2 * p + 1))
            rows = slice(2 * per * p, 2 * per * (p + 1))
            out[rows, :half] = jnp.concatenate([a[:per], b[:per]], axis=0).astype(BF16)
            out[rows, half:] = jnp.concatenate([a[per:], b[per:]], axis=0).astype(BF16)

    t_begin, t_forward, t_across, t_end = gather(tbuf)
    c_begin, c_forward, c_across, c_end = gather(cbuf)
    t_begin()
    t_forward()
    c_begin()
    t_across()
    c_forward()
    t_end()
    unpack(tbuf, xw)
    save(0).start()
    gate[...] = jnp.zeros_like(gate)
    up[...] = jnp.zeros_like(up)

    def first(k, carry):
        cols = pl.ds(pl.multiple_of(k * kc, kc), kc)
        gate_copy(k).wait()
        up_copy(k).wait()
        x = xw[:, cols]
        for w, e, acc in ((gw, gm, gate), (uw, um, up)):
            for b in range(kc // BLK):
                rows = pl.ds(pl.multiple_of(k * kc + b * BLK, BLK), BLK)
                w[rows, :] = masked(
                    w[rows, :], [e[j, k * (kc // BLK) + b] for j in range(hidden // BLK)]
                )
            acc[...] += dot(x, w[cols, :])
        return carry

    lax.fori_loop(0, kc_n // 2, first, 0)
    c_across()
    lax.fori_loop(kc_n // 2, kc_n, first, 0)

    step = 32

    def middle(k, carry):
        rows = pl.ds(pl.multiple_of(k * step, step), step)
        g, u = gate[rows, :], up[rows, :]
        s = jax.nn.sigmoid(g)
        a = g * s
        gs[rows, :] = a
        hid[rows, :] = (a * u).astype(BF16)
        du[rows, :] = u * s * (1.0 + g * (1.0 - s))
        return carry

    lax.fori_loop(0, total // step, middle, 0)
    c_end()
    unpack(cbuf, cw)
    save(1).start()
    save(2).start()

    sums = []

    def scatter_begin(which, k, low, high):
        parts = jnp.concatenate([low.reshape(n, per, h), high.reshape(n, per, h)], axis=1)
        pb[which, k] = parts.astype(BF16).reshape(2, 2, m, 2 * per, h)
        a = remote(pb.at[which, k, 1 - c], ra.at[which, k], c_peer)
        b = remote(bb.at[which, k], rb.at[which, k], y_peer)
        zs = [
            remote(cb.at[which, k, z_peers[off]], rz.at[which, k, off - 1], device(c, y, z_peers[off]))
            for off in range(1, m)
        ]
        a.start()

        def second():
            a.wait_recv()
            bb[which, k] = (pb[which, k, c, 1 - y].astype(F32) + ra[which, k, 1 - y].astype(F32)).astype(BF16)
            b.start()

        def third():
            b.wait_recv()
            cb[which, k] = (
                pb[which, k, c, y].astype(F32) + ra[which, k, y].astype(F32) + rb[which, k].astype(F32)
            ).astype(BF16)
            for copy in zs:
                copy.start()

        def last():
            value = (
                pb[which, k, c, y, z].astype(F32) + ra[which, k, y, z].astype(F32) + rb[which, k, z].astype(F32)
            )
            for off in range(1, m):
                zs[off - 1].wait_recv()
                value = value + rz[which, k, off - 1].astype(F32)
            out = gt_o if which else mixed_o
            out[:, k * width:k * width + h] = value[:per].astype(BF16)
            out[:, k * width + h:(k + 1) * width] = value[per:].astype(BF16)

        sums.append((second, third, last))

    def advance(i):
        for stage in range(2):
            j = i - 1 - stage
            if 0 <= j < 2 * CHUNKS:
                sums[j][stage]()

    for k in range(CHUNKS):
        down_copy(k).wait()
        cols = slice(k * width, (k + 1) * width)
        for j in range(hidden // BLK):
            rows = slice(j * BLK, (j + 1) * BLK)
            dw[k, rows, :] = masked(
                dw[k, rows, :], [dm[j, k * (width // BLK) + b] for b in range(width // BLK)]
            )
        hv = hid[...]
        scatter_begin(0, k, dot(hv, dw[k, :, :h]), dot(hv, dw[k, :, h:]))
        value = dot(cw[:, cols], dw[k], 1, 1)
        gh[...] = value if k == 0 else gh[...] + value
        advance(k)

    def pre(k, carry):
        rows = pl.ds(pl.multiple_of(k * step, step), step)
        g = gh[rows, :]
        ggp[rows, :] = (g * du[rows, :]).astype(BF16)
        gup[rows, :] = (g * gs[rows, :]).astype(BF16)
        return carry

    lax.fori_loop(0, total // step, pre, 0)
    save(3).start()
    save(4).start()

    for k in range(CHUNKS):
        a, b = ggp[...], gup[...]
        halves = []
        for o in (k * width, k * width + h):
            halves.append(dot(a, gw[o:o + h, :], 1, 1) + dot(b, uw[o:o + h, :], 1, 1))
        scatter_begin(1, k, *halves)
        advance(CHUNKS + k)
    for i in range(2 * CHUNKS, 2 * CHUNKS + 2):
        advance(i)
    for stages in sums:
        stages[2]()
    for copy, ok in sent:
        when(ok, copy.wait_send)
    for i in range(5):
        save(i).wait()


def grads_kernel(xw, cw, hid, ggp, gup, gm, um, dm, mixed, gt, gg, gu, gd, mixed_o, gt_o):
    i = pl.program_id(0)
    block = xw.shape[1]
    count = block // BLK

    @pl.when(i == 0)
    def _():
        mixed_o[...] = mixed[...]
        gt_o[...] = gt[...]

    def keep(value, scalars):
        wide = [jnp.full((8, BLK), v, jnp.int32).astype(F32) for v in scalars]
        wide = jnp.concatenate(wide, axis=1)
        cols = wide.shape[1]
        return (value.reshape(BLK // 8, 8, cols) * wide[None]).reshape(BLK, cols).astype(BF16)

    for pre, e, out in ((ggp, gm, gg), (gup, um, gu)):
        for b in range(count):
            rows = slice(b * BLK, (b + 1) * BLK)
            value = dot(xw[:, rows], pre[...], 0, 0)
            out[rows, :] = keep(value, [e[j, i * count + b] for j in range(e.shape[0])])
    for j in range(dm.shape[0]):
        rows = slice(j * BLK, (j + 1) * BLK)
        value = dot(hid[:, rows], cw[...], 0, 0)
        gd[rows, :] = keep(value, [dm[j, i * count + b] for b in range(count)])


def shards(n, tokens, cotangent, gate_weight, up_weight, down_weight, gate_mask, up_mask, down_mask):
    m = n // 4
    per, d = tokens.shape
    total = n * per
    hidden = gate_weight.shape[1]
    width = d // CHUNKS
    h = width // 2
    kc_n = 8
    copies = 2 * (8 * (m - 1) + 3) + 2 * CHUNKS * (m + 1)
    vmem = pl.BlockSpec(memory_space=pltpu.VMEM)
    hbm = pl.BlockSpec(memory_space=pl.ANY)
    smem = pl.BlockSpec(memory_space=pltpu.SMEM)
    gate_mask, up_mask = gate_mask.T, up_mask.T
    shape = jax.ShapeDtypeStruct
    mixed, grad_tokens, xw, cw, hid, ggp, gup = pl.pallas_call(
        functools.partial(exchange_kernel, m),
        out_shape=(
            shape((per, d), BF16), shape((per, d), BF16),
            shape((total, d), BF16), shape((total, d), BF16),
            shape((total, hidden), BF16), shape((total, hidden), BF16), shape((total, hidden), BF16),
        ),
        in_specs=[vmem] * 2 + [smem] * 3 + [hbm] * 3,
        out_specs=(vmem,) * 2 + (hbm,) * 5,
        scratch_shapes=[
            *[pltpu.VMEM((total, d), BF16)] * 2, *[pltpu.VMEM((total, hidden), BF16)] * 3,
            pltpu.VMEM((d, hidden), BF16), pltpu.VMEM((d, hidden), BF16),
            pltpu.VMEM((CHUNKS, hidden, width), BF16),
            pltpu.VMEM((2, 2, m, 2 * per, d // 2), BF16), pltpu.VMEM((2, 2, m, 2 * per, d // 2), BF16),
            *[pltpu.VMEM((total, hidden), F32)] * 5,
            pltpu.VMEM((2, CHUNKS, 2, 2, m, 2 * per, h), BF16),
            pltpu.VMEM((2, CHUNKS, 2, m, 2 * per, h), BF16),
            pltpu.VMEM((2, CHUNKS, m, 2 * per, h), BF16),
            pltpu.VMEM((2, CHUNKS, m, 2 * per, h), BF16),
            pltpu.VMEM((2, CHUNKS, m, 2 * per, h), BF16),
            pltpu.VMEM((2, CHUNKS, m - 1, 2 * per, h), BF16),
            pltpu.SemaphoreType.DMA((3, kc_n)),
            pltpu.SemaphoreType.DMA((5,)),
            pltpu.SemaphoreType.DMA((copies,)),
            pltpu.SemaphoreType.DMA((copies,)),
        ],
        compiler_params=pltpu.CompilerParams(
            collective_id=0, has_side_effects=True, vmem_limit_bytes=60 * 2**20
        ),
        cost_estimate=pl.CostEstimate(
            flops=12 * total * d * hidden, bytes_accessed=6 * d * hidden, transcendentals=total * hidden
        ),
    )(tokens, cotangent, gate_mask, up_mask, down_mask, gate_weight, up_weight, down_weight)

    block = 256
    whole = lambda *dims: pl.BlockSpec(dims, lambda i: (0, 0))
    grad_gate, grad_up, grad_down, mixed, grad_tokens = pl.pallas_call(
        grads_kernel,
        grid=(d // block,),
        out_shape=(shape((d, hidden), BF16), shape((d, hidden), BF16), shape((hidden, d), BF16),
                   shape((per, d), BF16), shape((per, d), BF16)),
        in_specs=[
            pl.BlockSpec((total, block), lambda i: (0, i)),
            pl.BlockSpec((total, block), lambda i: (0, i)),
            whole(total, hidden), whole(total, hidden), whole(total, hidden),
            smem, smem, smem, whole(per, d), whole(per, d),
        ],
        out_specs=(
            pl.BlockSpec((block, hidden), lambda i: (i, 0)),
            pl.BlockSpec((block, hidden), lambda i: (i, 0)),
            pl.BlockSpec((hidden, block), lambda i: (0, i)),
            whole(per, d), whole(per, d),
        ),
        compiler_params=pltpu.CompilerParams(vmem_limit_bytes=60 * 2**20),
        cost_estimate=pl.CostEstimate(
            flops=6 * total * d * hidden, bytes_accessed=6 * d * hidden, transcendentals=0
        ),
    )(xw, cw, hid, ggp, gup, gate_mask, up_mask, down_mask, mixed, grad_tokens)
    return mixed, grad_tokens, grad_gate, grad_up, grad_down


def solution(mesh):
    return jax.shard_map(
        functools.partial(shards, mesh.shape["tensor"]),
        mesh=mesh,
        in_specs=(
            P(("groups", "tensor"), None),
            P(("groups", "tensor"), None),
            P(None, "tensor"),
            P(None, "tensor"),
            P("tensor", None),
            P(None, "tensor"),
            P(None, "tensor"),
            P("tensor", None),
        ),
        out_specs=(
            P(("groups", "tensor"), None),
            P(("groups", "tensor"), None),
            P("groups", "tensor"),
            P("groups", "tensor"),
            P(("groups", "tensor"), None),
        ),
        check_vma=False,
    )
```
